32 devices in a mesh: dp: 16 (over z, y, x), head: 2 (over core).
Axes of the slice: x: 2, y: 2, z: 4, core: 2. Of those that a mesh axis runs over, the one named last changes fastest.
Arguments:
- frames: bfloat16 [2, 8192, 768], P(None, ('dp', 'head')), may hold values from -6 to 6
- text_states: bfloat16 [2, 16, 4, 256, 768], P(None, 'dp'), may hold values from -6 to 6
- cotangent: bfloat16 [2, 8192, 768], P(None, ('dp', 'head')), may hold values from -6 to 6
- item_lengths: int32 [2, 16, 4], P(None, 'dp'), may hold values from 0 to 512, as said below
- text_lengths: int32 [2, 16, 4], P(None, 'dp'), may hold values from 1 to 256, as said below
- timesteps: int32 [2, 16, 4], P(None, 'dp'), may hold values from 0 to 999
- w_qkv: bfloat16 [768, 2304], P(('dp', 'head')), may hold values from -0.21875 to 0.21875
- w_proj: bfloat16 [768, 768], P(('dp', 'head')), may hold values from -0.625 to 0.625
- w_query: bfloat16 [768, 768], P(('dp', 'head')), may hold values from -0.21875 to 0.21875
- w_cproj: bfloat16 [768, 768], P(('dp', 'head')), may hold values from -0.625 to 0.625
- w_ada: bfloat16 [768, 6912], P(('dp', 'head')), may hold values from -0.21875 to 0.21875
- b_ada: bfloat16 [6912], P(('dp', 'head')), may hold values from -3 to 3
- w_kv: bfloat16 [2, 768, 768], P(None, 'dp', 'head'), may hold values from -0.21875 to 0.21875
- w_up: bfloat16 [768, 3072], P('dp', 'head'), may hold values from -0.21875 to 0.21875
- w_down: bfloat16 [3072, 768], P('head', 'dp'), may hold values from -0.109375 to 0.109375
Outputs:
- block_out: float32 [2, 8192, 768], P(None, ('dp', 'head'))
- frames_grad: float32 [2, 8192, 768], P(None, ('dp', 'head'))
- text_grad: float32 [2, 16, 4, 256, 768], P(None, 'dp', None, 'head')
- qkv_grad: float32 [768, 2304], P(('dp', 'head'))
- proj_grad: float32 [768, 768], P(('dp', 'head'))
- query_grad: float32 [768, 768], P(('dp', 'head'))
- cproj_grad: float32 [768, 768], P(('dp', 'head'))
- ada_grad: float32 [768, 6912], P(('dp', 'head'))
- ada_bias_grad: float32 [6912], P(('dp', 'head'))
- kv_grad: float32 [2, 768, 768], P(None, 'dp', 'head')
- up_grad: float32 [768, 3072], P('dp', 'head')
- down_grad: float32 [3072, 768], P('head', 'dp')
The draws below stay inside these ranges and needn't reach their ends.
Inputs may be any that keep to these rules, and one draw needn't show every extreme that they name: `item_lengths`: A slab holds 4, 2 or 1 items of nominal length 128, 256 or 512 in its first slots, the other slots 0; an item's length lies between half its nominal length and that length, the first item of a slab has its nominal length, and every index of dp holds a single item of nominal length 512 in some micro-batch. `text_lengths`: the first slot of every slab has 256 live rows.
All inputs are finite; a program needn't handle non-finite values.
Results may differ from the reference program's by a relative error of at most 0.02.
Values may be sent and summed in bfloat16 or wider, within the bound.
No kernel may reach another device: no remote copies, remote signals or barrier semaphores. Data moves between devices by JAX's collectives and lax.ppermute only.
A program may use at most 256 MiB of HBM per device.

```python
import math
import jax
import jax.numpy as jnp
from jax import lax

D = 768
HEADS = 12
DH = 64
FF = 3072
TXT = 256
ITEMS = 4
SLAB = 512
MB = 2
CHIPS = 16
FRAMES = 8192


def draw_item_lengths(key, part):
    key = jax.random.fold_in(key, 11)
    bucket_key, forced_key, length_key = jax.random.split(key, 3)
    bucket = jax.random.randint(bucket_key, (MB, CHIPS), 0, 3)
    forced = jax.random.randint(forced_key, (CHIPS,), 0, MB)
    bucket = jnp.where(jnp.arange(MB)[:, None] == forced[None, :], 2, bucket)
    item_count = jnp.right_shift(jnp.int32(ITEMS), bucket.astype(jnp.int32))
    nominal = SLAB // item_count
    raw_draw = jax.random.randint(length_key, (MB, CHIPS, ITEMS), 0, 1 << 20)
    span_size = nominal // 2 + 1
    drawn = (nominal // 2)[..., None] + raw_draw % span_size[..., None]
    slot_index = jnp.arange(ITEMS)
    drawn = jnp.where(slot_index[None, None, :] == 0, nominal[..., None], drawn)
    return jnp.where(slot_index[None, None, :] < item_count[..., None], drawn, 0).astype(jnp.int32)


def draw_text_lengths(key, part):
    key = jax.random.fold_in(key, 23)
    drawn = jax.random.randint(key, (MB, CHIPS, ITEMS), 1, TXT + 1)
    slot_index = jnp.arange(ITEMS)
    return jnp.where(slot_index[None, None, :] == 0, TXT, drawn).astype(jnp.int32)


def touch_ends(values, key, smallest, largest):
    longest = values.shape.index(max(values.shape))
    spots = []
    for shift in (0, 1):
        where = [jax.random.randint(jax.random.fold_in(key, axis), (), 0, length) for axis, length in enumerate(values.shape)]
        where[longest] = (where[longest] + shift) % values.shape[longest]
        spots.append(tuple(where))
    return values.at[spots[0]].set(smallest).at[spots[1]].set(largest)


def levels(stream_key, dims, shards, low, top_value):
    gain = 1.0
    for dim, parts in shards:
        steps = jax.random.uniform(jax.random.fold_in(jax.random.fold_in(stream_key, 6), dim), (parts,), jnp.float32, low / len(shards), top_value / len(shards))
        gain = gain * jnp.repeat(jnp.exp(steps), dims[dim] // parts).reshape((-1,) + (1,) * (len(dims) - 1 - dim))
    return gain


def centred(own_key, extent, deviation, bound, pieces=(), kind=jnp.bfloat16):
    array = jax.random.normal(own_key, extent, jnp.float32) * deviation
    if len(pieces) > 0:
        array = levels(own_key, extent, pieces, -0.22, 0.18) * array
    return jnp.clip(array, min=-bound, max=bound).astype(kind)


def setup_inputs(seed: int = 0) -> dict:
    seeds = jax.random.split(jax.random.key(seed), 16)
    frames = centred(seeds[0], (MB, FRAMES, D), 1.0, 6.0, ((1, 32),))
    text_states = centred(seeds[1], (MB, CHIPS, ITEMS, TXT, D), 1.0, 6.0, ((1, 16),))
    cotangent = centred(seeds[2], (MB, FRAMES, D), 1.0, 6.0, ((1, 32),))
    item_lengths = draw_item_lengths(jax.random.fold_in(seeds[15], 71), 0)
    text_lengths = draw_text_lengths(jax.random.fold_in(seeds[15], 71), 0)
    timesteps = touch_ends(jax.random.randint(seeds[5], (MB, CHIPS, ITEMS), 0, 1000), jax.random.fold_in(seeds[5], 1), 0, 999).astype(jnp.int32)
    w_qkv = centred(seeds[6], (D, 3 * D), D ** -0.5, 0.21875, ((0, 32),))
    w_proj = centred(seeds[7], (D, D), (D // 8) ** -0.5, 0.625, ((0, 32),))
    w_query = centred(seeds[8], (D, D), D ** -0.5, 0.21875, ((0, 32),))
    w_cproj = centred(seeds[9], (D, D), (D // 8) ** -0.5, 0.625, ((0, 32),))
    w_ada = centred(seeds[10], (D, 9 * D), D ** -0.5, 0.21875, ((0, 32),))
    b_ada = centred(seeds[11], (9 * D,), 0.5, 3.0, ((0, 32),))
    w_kv = centred(seeds[12], (2, D, D), D ** -0.5, 0.21875, ((1, 16), (2, 2)))
    w_up = centred(seeds[13], (D, FF), D ** -0.5, 0.21875, ((0, 16), (1, 2)))
    w_down = centred(seeds[14], (FF, D), FF ** -0.5, 0.109375, ((0, 2), (1, 16)))
    return dict(frames=frames, text_states=text_states, cotangent=cotangent, item_lengths=item_lengths, text_lengths=text_lengths, timesteps=timesteps, w_qkv=w_qkv, w_proj=w_proj, w_query=w_query, w_cproj=w_cproj, w_ada=w_ada, b_ada=b_ada, w_kv=w_kv, w_up=w_up, w_down=w_down)


@jax.custom_vjp
def low(v):
    return lax.optimization_barrier(v.astype(jnp.bfloat16)).astype(jnp.float32)

@jax.custom_vjp
def low_back(v):
    return v

def low_keep(v):
    return (low(v), None)

def low_pass(kept, grad):
    return (grad,)

def back_keep(v):
    return (v, None)

def back_low(kept, grad):
    return (low(grad),)
low.defvjp(low_keep, low_pass)
low_back.defvjp(back_keep, back_low)
PRECISE = lax.Precision.HIGHEST

def product(left, right):
    return jnp.dot(left, right, precision=PRECISE, preferred_element_type=jnp.float32)

def layer_norm(values):
    center = values - lax.optimization_barrier(jnp.mean(values, axis=-1, keepdims=True))
    spread = lax.optimization_barrier(jnp.mean(center * center, axis=-1, keepdims=True))
    return center * lax.rsqrt(spread + 1e-06)

def gelu_tanh(values):
    return jax.nn.gelu(values, approximate=True)

def time_embed(timesteps, width):
    halfwidth = width // 2
    frequency = jnp.exp(-math.log(10000.0) * jnp.arange(halfwidth).astype(jnp.float32) / halfwidth)
    angles = timesteps.astype(jnp.float32)[:, None] * frequency[None, :]
    return jnp.concatenate([jnp.cos(angles), jnp.sin(angles)], axis=-1)

def slab_layout(lengths):
    item_count = jnp.sum((lengths > 0).astype(jnp.int32))
    nominal = SLAB // item_count
    position = jnp.arange(SLAB, dtype=jnp.int32)
    item_slot = position // nominal
    one_hot = item_slot[:, None] == jnp.arange(ITEMS, dtype=jnp.int32)[None, :]
    own_length = lax.optimization_barrier(jnp.sum(jnp.where(one_hot, lengths[None, :], 0), axis=1))
    frame_live = position - item_slot * nominal < own_length
    return (item_slot, one_hot.astype(jnp.float32), frame_live)

def text_layout(text_lengths):
    position = jnp.arange(ITEMS * TXT, dtype=jnp.int32)
    text_slot = position // TXT
    one_hot = text_slot[:, None] == jnp.arange(ITEMS, dtype=jnp.int32)[None, :]
    own_length = lax.optimization_barrier(jnp.sum(jnp.where(one_hot, text_lengths[None, :], 0), axis=1))
    return (text_slot, position % TXT < own_length)

def attention(queries, keys, values, query_slot, key_slot, key_live, heads):
    row_count = queries.shape[0]
    block_rows = min(512, row_count)
    score_scale = DH ** (-0.5)
    query_blocks = queries.reshape(row_count // block_rows, block_rows, heads, DH)
    slot_blocks = query_slot.reshape(row_count // block_rows, block_rows)
    key_heads = keys.reshape(keys.shape[0], heads, DH)
    value_heads = values.reshape(values.shape[0], heads, DH)

    def one_block(inputs):
        query_block, slot_block = inputs
        raw_score = jnp.einsum('qhd,khd->hqk', query_block, key_heads, precision=PRECISE) * score_scale
        scores = low_back(raw_score)
        allowed = (slot_block[:, None] == key_slot[None, :]) & key_live[None, :]
        weights = jax.nn.softmax(jnp.where(allowed[None], scores, -1e+30), axis=-1)
        output = jnp.einsum('hqk,khd->qhd', low(weights), value_heads, precision=PRECISE)
        return output.reshape(block_rows, heads * DH)
    return lax.map(jax.checkpoint(one_block), (query_blocks, slot_blocks)).reshape(row_count, heads * DH)

def forward_block(params, residual, text, lengths, text_lengths, timesteps):
    w_qkv, w_proj, w_query, w_cproj, w_ada, b_ada, w_kv, w_up, w_down = params
    frame_slot, frame_onehot, frame_live = slab_layout(lengths)
    text_slot, text_live = text_layout(text_lengths)
    embedding = jax.nn.silu(time_embed(timesteps, D))
    modulation = product(frame_onehot, product(embedding, w_ada) + b_ada)
    shift_one, scale_one, gate_one, shift_two, scale_two, gate_two, shift_three, scale_three, gate_three = jnp.split(modulation, 9, axis=1)
    normed_one = low(layer_norm(residual) * (1.0 + scale_one) + shift_one)
    projected = product(normed_one, w_qkv)
    queries, keys, values = [low_back(low(column_part)) for column_part in jnp.split(projected, 3, axis=1)]
    attended = low_back(low(attention(queries, keys, values, frame_slot, frame_slot, frame_live, HEADS)))
    branch_one = low_back(product(attended, w_proj))
    after_one = residual + gate_one * branch_one
    normed_two = low(layer_norm(after_one) * (1.0 + scale_two) + shift_two)
    cross_query = low_back(low(product(normed_two, w_query)))
    cross_keys = low_back(low(product(text, w_kv[0])))
    cross_values = low_back(low(product(text, w_kv[1])))
    crossed = low_back(low(attention(cross_query, cross_keys, cross_values, frame_slot, text_slot, text_live, HEADS)))
    branch_two = low_back(product(crossed, w_cproj))
    after_two = after_one + gate_two * branch_two
    normed_three = low(layer_norm(after_two) * (1.0 + scale_three) + shift_three)
    hidden_up = low_back(product(normed_three, w_up))
    activated = low(gelu_tanh(hidden_up))
    branch_three = low_back(product(activated, w_down))
    return after_two + gate_three * branch_three

def reference(frames, text_states, cotangent, item_lengths, text_lengths, timesteps, w_qkv, w_proj, w_query, w_cproj, w_ada, b_ada, w_kv, w_up, w_down):
    params = tuple((weight.astype(jnp.float32) for weight in (w_qkv, w_proj, w_query, w_cproj, w_ada, b_ada, w_kv, w_up, w_down)))
    slabs = MB * CHIPS
    frame_rows = frames.astype(jnp.float32).reshape(slabs, SLAB, D)
    text_rows = text_states.astype(jnp.float32).reshape(slabs, ITEMS * TXT, D)
    grad_rows = cotangent.astype(jnp.float32).reshape(slabs, SLAB, D)
    length_rows = item_lengths.reshape(slabs, ITEMS)
    text_length_rows = text_lengths.reshape(slabs, ITEMS)
    step_rows = timesteps.reshape(slabs, ITEMS)

    def one_slab(totals, inputs):
        slab_frames, slab_text, slab_grad, slab_lengths, slab_text_lengths, slab_steps = inputs

        def apply_block(weights, frame_part, text_part):
            return forward_block(weights, frame_part, text_part, slab_lengths, slab_text_lengths, slab_steps)
        output, pullback = jax.vjp(apply_block, params, slab_frames, slab_text)
        weight_grads, frame_grad, text_grad = pullback(slab_grad)
        totals = jax.tree.map(lambda former, latter: former + latter, totals, weight_grads)
        return (totals, (output, frame_grad, text_grad))
    zero_grads = tuple((jnp.zeros_like(weight) for weight in params))
    totals, (outputs, frame_grads, text_grads) = lax.scan(one_slab, zero_grads, (frame_rows, text_rows, grad_rows, length_rows, text_length_rows, step_rows))
    return (outputs.reshape(MB, FRAMES, D), frame_grads.reshape(MB, FRAMES, D), text_grads.reshape(MB, CHIPS, ITEMS, TXT, D), totals[0], totals[1], totals[2], totals[3], totals[4], totals[5], totals[6], totals[7], totals[8])
```

```python
import functools
import math

import jax
import jax.numpy as jnp
from jax import lax
from jax.experimental import pallas as pl
from jax.experimental.pallas import tpu as pltpu
from jax.sharding import PartitionSpec as P

HEADS = 12
DH = 64
TXT = 256
ITEMS = 4
SLAB = 512
BLOCKS = 4
ROWS = SLAB // BLOCKS
PAIR = 2 * DH
SCALE = DH**-0.5
MASKED = -1e30
PLANE = 16

BF16 = jnp.bfloat16
F32 = jnp.float32
PRECISE = lax.Precision.HIGHEST
BOTH = ("dp", "head")


def params(mebibytes):
    return pltpu.CompilerParams(vmem_limit_bytes=mebibytes * 2**20)


def cost(microseconds):
    return pl.CostEstimate(
        flops=int(1.1e9 * microseconds), bytes_accessed=int(3.5e6 * microseconds), transcendentals=0
    )


def mm(left, right):
    return jnp.dot(left, right, preferred_element_type=F32)


def mm_tl(left, right):
    return lax.dot_general(left, right, (((0,), (0,)), ((), ())), preferred_element_type=F32)


def mm_tr(left, right):
    return lax.dot_general(left, right, (((1,), (1,)), ((), ())), preferred_element_type=F32)


def swap_core(values):
    return lax.ppermute(values, "head", [(0, 1), (1, 0)])


def hop(values, first_core, second_core):
    steps = (first_core, second_core)
    pairs = [(2 * d + c, 2 * (d ^ steps[c]) + c) for d in range(PLANE) for c in range(2)]
    return lax.ppermute(values, BOTH, pairs)


def cut_kernel(groups, core, *refs):
    ins, (kept, sent) = refs[:-2], refs[-2:]
    start = 0
    for source, count in zip(ins, groups):
        half = source.shape[1] // count // 2
        for at in range(count):
            for side, out in ((core[0], kept), (1 - core[0], sent)):
                cols = pl.ds(pl.multiple_of((2 * at + side) * half, 128), half)
                out[:, start : start + half] = source[:, cols]
            start += half


def cut(core, shards, groups):
    rows = shards[0].shape[0]
    width = sum(shard.shape[1] for shard in shards) // 2
    held = pl.BlockSpec(memory_space=pltpu.VMEM)
    return pl.pallas_call(
        functools.partial(cut_kernel, groups),
        out_shape=[jax.ShapeDtypeStruct((rows, width), BF16)] * 2,
        in_specs=[pl.BlockSpec(memory_space=pltpu.SMEM)] + [held] * len(shards),
        out_specs=[held] * 2,
        compiler_params=params(8),
        cost_estimate=cost(1),
        name="cut",
    )(jnp.stack([core]).astype(jnp.int32), *shards)


def near_bits(core):
    return jnp.where(core == 0, 1, 2), jnp.where(core == 0, 2, 1)


def tie(value, *after):
    return lax.optimization_barrier((value,) + after)[0]


def place_kernel(starts, widths, dst, *refs):
    pieces, outs = refs[:4], refs[4:]
    for quarter in range(4):
        for step in range(4):
            at = dst[4 * quarter + step]
            for out, start, width in zip(outs, starts, widths):
                out[at] = pieces[quarter][step, :, start : start + width]


def place(dst, pieces, widths):
    _, rows, total = pieces[0].shape
    starts = [sum(widths[:i]) for i in range(len(widths))]
    held = pl.BlockSpec(memory_space=pltpu.VMEM)
    outs = pl.pallas_call(
        functools.partial(place_kernel, starts, widths),
        out_shape=[jax.ShapeDtypeStruct((PLANE, rows, width), BF16) for width in widths],
        in_specs=[pl.BlockSpec(memory_space=pltpu.SMEM)] + [held] * 4,
        out_specs=[held] * len(widths),
        compiler_params=params(16),
        cost_estimate=cost(1.5),
        name="place",
    )(dst.astype(jnp.int32), *pieces)
    return [out.reshape(PLANE * rows, width) for out, width in zip(outs, widths)]


class Gather:
    def __init__(self, shards, dp, core, n_dp):
        self.widths = [shard.shape[1] for shard in shards]
        self.mine = jnp.concatenate(shards, axis=1) if len(shards) > 1 else shards[0]
        self.hops = n_dp == PLANE
        near, far = near_bits(core)
        planes = dp ^ jnp.stack([jnp.zeros_like(near), near, far, near + far])
        self.order = (planes[:, None] ^ jnp.array([[0, 12, 4, 8]], jnp.int32)).reshape(-1)

    def z_far(self, *after):
        if self.hops:
            self.mine = tie(self.mine, *after) if after else self.mine
            self.far = hop(self.mine, 12, 12)

    def z_near(self, *after):
        self.two = self.first = self.second = self.mine
        if self.hops:
            far = tie(self.far, *after) if after else self.far
            self.two = jnp.stack([self.mine, far])
            self.got = hop(self.two, 4, 4)

    def landed(self, *after):
        if self.hops:
            got = tie(self.got, *after) if after else self.got
            self.first = jnp.concatenate([self.two, got], axis=0)

    def across(self, *after):
        if self.hops:
            first = tie(self.first, *after) if after else self.first
            self.second = hop(first, 1, 2)
            self.third = hop(first, 2, 1)

    def corner(self, *after):
        self.last = self.mine
        if self.hops:
            self.second, self.third = lax.optimization_barrier((self.second, self.third) + after)[:2]
            self.last = hop(self.second, 2, 1)

    def finish(self, *after):
        last = tie(self.last, *after) if after else self.last
        if self.hops:
            owns = place(self.order, [self.first, self.second, self.third, last], self.widths)
        else:
            whole = lax.all_gather(last, "dp", axis=0, tiled=True)
            cuts = [sum(self.widths[: i + 1]) for i in range(len(self.widths) - 1)]
            owns = jnp.split(whole, cuts, axis=1)
        return [(own, swap_core(own)) for own in owns]


def block_sum(counts, refs, extras, z):
    refs, start = list(refs), 0
    for count in counts:
        parts, refs = refs[:count], refs[count:]
        width = parts[0].shape[-1]
        cols = slice(start, start + width)
        value = sum(part[z, 0].astype(F32) for part in parts)
        for extra in extras:
            value = value + extra[0, z, :, cols].astype(F32)
        yield cols, value
        start += width


def add_kernel(counts, index, *refs):
    total = sum(counts)
    totals, extras, out = refs[:total], refs[total:-1], refs[-1]
    for z in range(4):
        for cols, value in block_sum(counts, totals, extras, z):
            out[0, z, :, cols] = value.astype(BF16)


def split_kernel(counts, index, *refs):
    total = sum(counts)
    totals, extras = refs[:total], refs[total:-3]
    send, kept, total_ref = refs[-3:]
    for z in range(4):
        for cols, value in block_sum(counts, totals, extras, z):
            total_ref[z, :, cols] = value
    for step in range(2):
        kept[step] = total_ref[index[1 + step]]
        send[step] = total_ref[index[3 + step]].astype(BF16)


def add_blocks(index, totals, extras, split):
    counts = [len(parts) for parts in totals]
    width = sum(parts[0].shape[3] for parts in totals)
    totals = [part for parts in totals for part in parts]
    rows = totals[0].shape[2]
    steps = 1 if split else index.shape[0]
    in_specs = [
        pl.BlockSpec((4, 1, rows, part.shape[3]), lambda j, idx: (0, idx[j], 0, 0)) for part in totals
    ]
    for _, at in extras:
        in_specs.append(pl.BlockSpec((1, 4, rows, width), lambda j, idx, at=at: (at, 0, 0, 0)))
    scratch = []
    if split:
        out_shape = [jax.ShapeDtypeStruct((2, rows, width), kind) for kind in (BF16, F32)]
        out_specs = [pl.BlockSpec((2, rows, width), lambda j, idx: (0, 0, 0))] * 2
        scratch = [pltpu.VMEM((4, rows, width), F32)]
    else:
        out_shape = jax.ShapeDtypeStruct((steps, 4, rows, width), BF16)
        out_specs = pl.BlockSpec((1, 4, rows, width), lambda j, idx: (j, 0, 0, 0))
    return pl.pallas_call(
        functools.partial(split_kernel if split else add_kernel, counts),
        out_shape=out_shape,
        grid_spec=pltpu.PrefetchScalarGridSpec(
            num_scalar_prefetch=1,
            grid=(steps,),
            in_specs=in_specs,
            out_specs=out_specs,
            scratch_shapes=scratch,
        ),
        compiler_params=params(18 if split else 14),
        cost_estimate=cost(steps * rows * width / 1e5),
        name="split_blocks" if split else "add_blocks",
    )(index.astype(jnp.int32), *totals, *[extra for extra, _ in extras])


class Scatter:
    def __init__(self, dp, core, n_dp):
        self.hops = n_dp == PLANE
        self.parts, self.totals = [], []
        if self.hops:
            near, far = near_bits(core)
            plane, self.deep = dp % 4, (dp // 4) ^ jnp.array([0, 3, 1, 2], jnp.int32)
            self.first = jnp.stack([plane ^ near, plane ^ near ^ far])
            self.second = jnp.stack([plane ^ far])
            self.third = jnp.stack([plane])

    def add(self, left, own, other):
        sent = mm_tl(left, other).astype(BF16)
        self.parts.append((left, own, swap_core(sent)))
        return sent

    def chip(self, *after):
        for left, own, got in self.parts:
            own = tie(own, *after) if after else own
            self.totals.append([(mm_tl(left, own) + got.astype(F32)).astype(BF16)])
        self.parts = []
        return [parts[0] for parts in self.totals]

    def across(self, *after):
        if not self.hops:
            self.total = jnp.concatenate([sum(parts) for parts in self.totals], axis=1)
            return self.total
        shape = lambda v: v.reshape(4, 4, v.shape[0] // PLANE, v.shape[1])
        if after:
            self.totals[0][0] = tie(self.totals[0][0], *after)
        self.totals = [[shape(part) for part in parts] for parts in self.totals]
        send = add_blocks(self.first, self.totals, [], False)
        self.near = hop(send, 1, 2)
        return send

    def corner(self, *after):
        if not self.hops:
            return self.total
        self.near = tie(self.near, *after)
        send = add_blocks(self.second, self.totals, [(self.near, 1)], False)
        self.far = hop(send, 2, 1)
        return send

    def z_near(self, *after):
        if not self.hops:
            return self.total
        far = tie(self.far, *after)
        index = jnp.concatenate([self.third, self.deep])
        send, self.kept = add_blocks(index, self.totals, [(self.near, 0), (far, 0)], True)
        self.got = hop(send, 4, 4)
        return send

    def z_far(self, *after):
        if not self.hops:
            return self.total
        got = tie(self.got, *after)
        self.sum = self.kept[0] + got[0].astype(F32)
        send = (self.kept[1] + got[1].astype(F32)).astype(BF16)
        self.got = hop(send, 12, 12)
        return send

    def finish(self, *after):
        if not self.hops:
            return lax.psum_scatter(self.total, "dp", scatter_dimension=0, tiled=True).astype(F32)
        got = tie(self.got, *after) if after else self.got
        return self.sum + got.astype(F32)


def lanes_of(head, rows):
    lane = lax.broadcasted_iota(jnp.int32, (rows, PAIR), 1)
    return (lane < DH) if head == 0 else (lane >= DH)


def stacked(values):
    zero = jnp.zeros_like(values)
    rows = values.shape[0]
    return jnp.concatenate([jnp.where(lanes_of(head, rows), values, zero) for head in range(2)], axis=0)


def unstacked(values):
    rows = values.shape[0] // 2
    return jnp.where(lanes_of(0, rows), values[:rows], values[rows:])


def attend(queries, keys, values, bias):
    scores = mm_tr(stacked(queries * BF16(SCALE)), keys) + bias
    weights = jnp.exp(scores - jnp.max(scores, axis=-1, keepdims=True))
    total = jnp.sum(weights, axis=-1, keepdims=True)
    return unstacked(mm(weights.astype(BF16), values) / total).astype(BF16)


def self_forward_kernel(q_ref, k_ref, v_ref, bias_ref, o_ref):
    chunk = 128
    keys, values = k_ref[...], v_ref[...]
    for start in range(0, SLAB, chunk):
        rows = slice(start, start + chunk)
        bias = bias_ref[rows, :]
        o_ref[rows, :] = attend(q_ref[rows, :], keys, values, jnp.concatenate([bias, bias], axis=0))


def self_forward(projected, bias):
    width = projected.shape[1] // 3
    pairs = width // PAIR
    whole = pl.BlockSpec((SLAB, SLAB), lambda j: (0, 0))
    part = lambda which: pl.BlockSpec((SLAB, PAIR), lambda j, w=which: (0, w * pairs + j))
    scores = 2 * pairs * SLAB * SLAB
    return pl.pallas_call(
        self_forward_kernel,
        out_shape=jax.ShapeDtypeStruct((SLAB, width), BF16),
        grid=(pairs,),
        in_specs=[part(0), part(1), part(2), whole],
        out_specs=pl.BlockSpec((SLAB, PAIR), lambda j: (0, j)),
        compiler_params=params(12),
        cost_estimate=cost(1.5 * pairs),
        name="self_forward",
    )(projected, projected, projected, bias)


def pull_back(queries, keys, values, grad, bias):
    queries = stacked(queries * BF16(SCALE))
    grad = stacked(grad)
    scores = mm_tr(keys, queries) + bias
    weights = jnp.exp(scores - jnp.max(scores, axis=0, keepdims=True))
    weights = weights * (1.0 / jnp.sum(weights, axis=0, keepdims=True))
    grad_weights = mm_tr(values, grad)
    inner = jnp.sum(weights * grad_weights, axis=0, keepdims=True)
    grad_scores = (weights * (grad_weights - inner)).astype(BF16)
    return (
        unstacked(mm_tl(grad_scores, keys)) * SCALE,
        mm(grad_scores, queries),
        mm(weights.astype(BF16), grad),
    )


def self_backward_kernel(meta, q_ref, k_ref, v_ref, g_ref, bias_ref, out_ref):
    chunk = 128
    pairs = out_ref.shape[1] // PAIR // 3
    pair = pl.program_id(0)
    keys, values = k_ref[...], v_ref[...]
    key_total = value_total = 0.0
    parts = []
    for start in range(0, SLAB, chunk):
        rows = slice(start, start + chunk)
        bias = bias_ref[:, rows]
        query_grad, key_grad, value_grad = pull_back(
            q_ref[rows, :], keys, values, g_ref[rows, :], jnp.concatenate([bias, bias], axis=1)
        )
        parts.append(query_grad)
        key_total = key_total + key_grad
        value_total = value_total + value_grad
    for which, grads in enumerate((jnp.concatenate(parts, axis=0), key_total, value_total)):
        cols = pl.ds(pl.multiple_of((which * pairs + pair) * PAIR, PAIR), PAIR)
        out_ref[:, cols] = grads.astype(BF16)


def self_backward(meta, projected, grad, bias):
    half = projected.shape[1] // 3
    pairs = half // PAIR
    part = lambda which: pl.BlockSpec((SLAB, PAIR), lambda j, m, w=which: (0, w * pairs + j))
    scores = 2 * pairs * SLAB * SLAB
    return pl.pallas_call(
        self_backward_kernel,
        out_shape=jax.ShapeDtypeStruct((SLAB, 3 * half), BF16),
        grid_spec=pltpu.PrefetchScalarGridSpec(
            num_scalar_prefetch=1,
            grid=(pairs,),
            in_specs=[
                part(0),
                part(1),
                part(2),
                pl.BlockSpec((SLAB, PAIR), lambda j, m: (0, m[BLOCKS] + j)),
                pl.BlockSpec((SLAB, SLAB), lambda j, m: (0, 0)),
            ],
            out_specs=pl.BlockSpec((SLAB, 3 * half), lambda j, m: (0, 0)),
        ),
        compiler_params=params(12),
        cost_estimate=cost(10),
        name="self_backward",
    )(meta, projected, projected, projected, grad, bias)


def cross_forward_kernel(meta, q_ref, k_ref, v_ref, bias_ref, o_ref):
    for block in range(BLOCKS):
        slot = meta[block]
        own = pl.ds(pl.multiple_of(slot * TXT, TXT), TXT)
        rows = slice(block * ROWS, (block + 1) * ROWS)
        o_ref[rows, :] = attend(q_ref[rows, :], k_ref[own, :], v_ref[own, :], bias_ref[slot])


def text_part(which, pairs, pair_at):
    def index(j, m):
        pair = pair_at(j, m)
        other = jnp.where(pair // pairs == m[BLOCKS] // pairs, 1, 0)
        return (0, (2 * other + which) * pairs + lax.rem(pair, pairs))

    return pl.BlockSpec((ITEMS * TXT, PAIR), index)


def cross_forward(meta, queries, text_kv, bias):
    width = queries.shape[1]
    pairs = width // PAIR
    frames = pl.BlockSpec((SLAB, PAIR), lambda j, m: (0, j))
    part = lambda which: text_part(which, pairs // 2, lambda j, m: j)
    scores = 2 * pairs * SLAB * TXT
    return pl.pallas_call(
        cross_forward_kernel,
        out_shape=jax.ShapeDtypeStruct((SLAB, width), BF16),
        grid_spec=pltpu.PrefetchScalarGridSpec(
            num_scalar_prefetch=1,
            grid=(pairs,),
            in_specs=[
                frames,
                part(0),
                part(1),
                pl.BlockSpec((ITEMS, 1, TXT), lambda j, m: (0, 0, 0)),
            ],
            out_specs=frames,
        ),
        compiler_params=params(8),
        cost_estimate=cost(7),
        name="cross_forward",
    )(meta, queries, text_kv, text_kv, bias)


def cross_backward_kernel(meta, q_ref, k_ref, v_ref, g_ref, bias_ref, dq_ref, dkv_ref, dk_acc, dv_acc):
    pairs = dkv_ref.shape[2] // PAIR // 2
    pair = lax.rem(pl.program_id(0), pairs)
    dk_acc[...] = jnp.zeros_like(dk_acc)
    dv_acc[...] = jnp.zeros_like(dv_acc)
    for block in range(BLOCKS):
        own = pl.ds(pl.multiple_of(meta[block] * TXT, TXT), TXT)
        rows = slice(block * ROWS, (block + 1) * ROWS)
        bias = bias_ref[own, :]
        query_grad, key_grad, value_grad = pull_back(
            q_ref[rows, :], k_ref[own, :], v_ref[own, :], g_ref[rows, :], jnp.concatenate([bias, bias], axis=1)
        )
        dq_ref[rows, :] = query_grad.astype(BF16)
        dk_acc[own, :] += key_grad
        dv_acc[own, :] += value_grad
    dkv_ref[0, :, pl.ds(pl.multiple_of(pair * PAIR, PAIR), PAIR)] = dk_acc[...].astype(BF16)
    dkv_ref[0, :, pl.ds(pl.multiple_of((pairs + pair) * PAIR, PAIR), PAIR)] = dv_acc[...].astype(BF16)


def cross_backward(meta, queries, text_kv, grad, bias):
    width = queries.shape[1]
    pairs = width // PAIR // 2
    pair_at = lambda j, m: lax.rem(m[BLOCKS] + j, 2 * pairs)
    frames = pl.BlockSpec((SLAB, PAIR), lambda j, m: (0, pair_at(j, m)))
    part = lambda which: text_part(which, pairs, pair_at)
    scores = 4 * pairs * SLAB * TXT
    return pl.pallas_call(
        cross_backward_kernel,
        out_shape=[
            jax.ShapeDtypeStruct((SLAB, width), BF16),
            jax.ShapeDtypeStruct((2, ITEMS * TXT, width), BF16),
        ],
        grid_spec=pltpu.PrefetchScalarGridSpec(
            num_scalar_prefetch=1,
            grid=(2 * pairs,),
            in_specs=[
                frames,
                part(0),
                part(1),
                frames,
                pl.BlockSpec((ITEMS * TXT, ROWS), lambda j, m: (0, 0)),
            ],
            out_specs=[
                frames,
                pl.BlockSpec((1, ITEMS * TXT, width), lambda j, m: (1 - j // pairs, 0, 0)),
            ],
            scratch_shapes=[pltpu.VMEM((ITEMS * TXT, PAIR), F32)] * 2,
        ),
        compiler_params=params(12),
        cost_estimate=cost(13.6),
        name="cross_backward",
    )(meta, queries, text_kv, text_kv, grad, bias)


def normed(values):
    center = values - jnp.mean(values, axis=-1, keepdims=True)
    spread = lax.rsqrt(jnp.mean(center * center, axis=-1, keepdims=True) + 1e-06)
    return center * spread, spread


def by_block(values):
    return values.reshape(BLOCKS, ROWS, -1)


def flat(values):
    return values.reshape(SLAB, -1)


def block_at(j, m):
    return lax.rem(2 * m[0] + j, BLOCKS)


def block_specs(width):
    rows = pl.BlockSpec((ROWS, width), lambda j, m: (block_at(j, m), 0))
    mod = lambda which: pl.BlockSpec((1, 1, width), lambda j, m, w=which: (block_at(j, m), 0, w))
    sums = lambda count: pl.BlockSpec((1, count, width), lambda j, m: (block_at(j, m), 0, 0))
    split = [
        pl.BlockSpec((ROWS, width), lambda j, m: (jnp.minimum(j, 1), 0)),
        pl.BlockSpec((ROWS, width), lambda j, m: (jnp.maximum(j - 2, 0), 0)),
    ]
    return rows, mod, sums, split


def write_split(values, kept, sent):
    step = pl.program_id(0)

    @pl.when(step < 2)
    def _():
        kept[...] = values

    @pl.when(step >= 2)
    def _():
        sent[...] = values


def top_kernel(meta, dy_ref, x_ref, branch_ref, gate_ref, kept, sent, grad_ref, sum_ref):
    dy, branch, gate = dy_ref[...].astype(F32), branch_ref[...], gate_ref[0]
    write_split(x_ref[...] + gate * branch, kept, sent)
    grad_ref[...] = (dy * gate).astype(BF16)
    sum_ref[0] = jnp.sum(dy * branch, axis=0, keepdims=True)


def top_stage(meta, grad_out, values, branch, mods):
    width = values.shape[1]
    rows, mod, sums, split = block_specs(width)
    half_shape = jax.ShapeDtypeStruct((SLAB // 2, width), F32)
    return pl.pallas_call(
        top_kernel,
        out_shape=[
            half_shape,
            half_shape,
            jax.ShapeDtypeStruct((SLAB, width), BF16),
            jax.ShapeDtypeStruct((BLOCKS, 1, width), F32),
        ],
        grid_spec=pltpu.PrefetchScalarGridSpec(
            num_scalar_prefetch=1,
            grid=(BLOCKS,),
            in_specs=[rows, rows, rows, mod(8)],
            out_specs=split + [rows, sums(1)],
        ),
        compiler_params=params(8),
        cost_estimate=cost(1),
        name="top_stage",
    )(meta, grad_out, values, branch, mods)


def norm_back(grad, values, scale_by):
    norm, spread = normed(values)
    inner = grad * (1.0 + scale_by)
    back = (
        inner
        - jnp.mean(inner, axis=-1, keepdims=True)
        - norm * jnp.mean(inner * norm, axis=-1, keepdims=True)
    ) * spread
    return back, jnp.sum(grad, axis=0, keepdims=True), jnp.sum(grad * norm, axis=0, keepdims=True)


def middle_kernel(meta, d_ref, x_ref, old_ref, branch_ref, scale_ref, gate_ref, total_ref, grad_ref, sum_ref):
    back, shift_sum, scale_sum = norm_back(d_ref[...], x_ref[...], scale_ref[0])
    total = old_ref[...].astype(F32) + back
    total_ref[...] = total
    grad_ref[...] = (total * gate_ref[0]).astype(BF16)
    gate_sum = jnp.sum(total * branch_ref[...], axis=0, keepdims=True)
    sum_ref[0] = jnp.concatenate([shift_sum, scale_sum, gate_sum], axis=0)


def middle_stage(meta, grad, values, old, branch, mods, which):
    width = values.shape[1]
    rows, mod, sums, _ = block_specs(width)
    return pl.pallas_call(
        middle_kernel,
        out_shape=[
            jax.ShapeDtypeStruct((SLAB, width), F32),
            jax.ShapeDtypeStruct((SLAB, width), BF16),
            jax.ShapeDtypeStruct((BLOCKS, 3, width), F32),
        ],
        grid_spec=pltpu.PrefetchScalarGridSpec(
            num_scalar_prefetch=1,
            grid=(BLOCKS,),
            in_specs=[rows, rows, rows, rows, mod(3 * which + 1), mod(3 * which - 1)],
            out_specs=[rows, rows, sums(3)],
        ),
        compiler_params=params(10),
        cost_estimate=cost(2),
        name="middle_stage",
    )(meta, grad, values, old, branch, mods, mods)


def bottom_kernel(meta, d_ref, x_ref, old_ref, scale_ref, kept, sent, sum_ref):
    back, shift_sum, scale_sum = norm_back(d_ref[...], x_ref[...].astype(F32), scale_ref[0])
    write_split(old_ref[...] + back, kept, sent)
    sum_ref[0] = jnp.concatenate([shift_sum, scale_sum], axis=0)


def bottom_stage(meta, grad, values, old, mods):
    width = values.shape[1]
    rows, mod, sums, split = block_specs(width)
    half_shape = jax.ShapeDtypeStruct((SLAB // 2, width), F32)
    return pl.pallas_call(
        bottom_kernel,
        out_shape=[half_shape, half_shape, jax.ShapeDtypeStruct((BLOCKS, 2, width), F32)],
        grid_spec=pltpu.PrefetchScalarGridSpec(
            num_scalar_prefetch=1,
            grid=(BLOCKS,),
            in_specs=[rows, rows, rows, mod(1)],
            out_specs=split + [sums(2)],
        ),
        compiler_params=params(8),
        cost_estimate=cost(2),
        name="bottom_stage",
    )(meta, grad, values, old, mods)


ROOT = math.sqrt(2.0 / math.pi)


def gelu_parts(values):
    square = values * values
    bent = jnp.tanh(ROOT * values * (1.0 + 0.044715 * square))
    slope = 0.5 * (1.0 + bent) + 0.5 * values * (1.0 - bent * bent) * (
        ROOT * (1.0 + 3.0 * 0.044715 * square)
    )
    return 0.5 * values * (1.0 + bent), slope


def time_embed(timesteps, width):
    halfwidth = width // 2
    frequency = jnp.exp(-math.log(10000.0) * jnp.arange(halfwidth).astype(F32) / halfwidth)
    angles = timesteps.astype(F32)[:, None] * frequency[None, :]
    return jax.nn.silu(jnp.concatenate([jnp.cos(angles), jnp.sin(angles)], axis=-1))


def time_features(timesteps, feature, width):
    halfwidth = width // 2
    place = jnp.where(feature < halfwidth, feature, feature - halfwidth)
    frequency = jnp.exp(-math.log(10000.0) * place.astype(F32) / halfwidth)
    angles = timesteps.astype(F32)[:, None] * frequency
    return jax.nn.silu(jnp.where(feature < halfwidth, jnp.cos(angles), jnp.sin(angles)))


def per_device(
    frames,
    text_states,
    cotangent,
    item_lengths,
    text_lengths,
    timesteps,
    w_qkv,
    w_proj,
    w_query,
    w_cproj,
    w_ada,
    b_ada,
    w_kv,
    w_up,
    w_down,
):
    n_dp = lax.axis_size("dp")
    n_all = n_dp * lax.axis_size("head")
    dp, core = lax.axis_index("dp"), lax.axis_index("head")
    width = frames.shape[2]
    half = width // 2
    thin = w_qkv.shape[0]

    def pick(pair):
        return jnp.where(core == 0, pair[0], pair[1])

    def join(own, other, axis):
        return jnp.where(
            core == 0,
            jnp.concatenate([own, other], axis=axis),
            jnp.concatenate([other, own], axis=axis),
        )

    def part(values, size, which, axis):
        return lax.dynamic_slice_in_dim(values, which * size, size, axis)

    def own_frames(values):
        kept, sent = pick((values[0], values[1])), pick((values[1], values[0]))
        return join(kept, swap_core(sent), 0)

    def halves(values, axis):
        low, high = jnp.split(values, 2, axis=axis)
        return pick((low, high)), swap_core(pick((high, low)))

    def both(kept, got):
        return join(kept[None], got[None], 0)

    gather = lambda *shards: Gather(shards, dp, core, n_dp)
    kept_half, sent = cut(core, [w_qkv, w_proj, w_query, w_cproj], [3, 1, 1, 1])
    got = swap_core(sent)

    lane_tiles = w_ada.shape[1] // 128
    ada_cols = 128 * (-(-lane_tiles // n_all))
    owners = w_ada.shape[1] // ada_cols
    bias_cols = b_ada.shape[0]
    steps_here = timesteps.reshape(1, -1)
    coded = jnp.concatenate([steps_here // 32, steps_here % 32], axis=1).astype(BF16)
    coded = jnp.concatenate(
        [
            jnp.pad(coded, ((0, 0), (0, ada_cols - coded.shape[1]))),
            jnp.pad(b_ada[None], ((0, 0), (0, ada_cols - bias_cols))),
        ],
        axis=0,
    )
    packed = tie(w_ada, sent).reshape(thin, owners, ada_cols).transpose(1, 0, 2)
    packed = jnp.concatenate(
        [
            jnp.pad(packed, ((0, n_all - owners), (0, 0), (0, 0))),
            jnp.broadcast_to(coded[None], (n_all,) + coded.shape),
        ],
        axis=1,
    )
    shared = join(kept_half, tie(got, packed), 0)
    qkv_shard, proj_shard, query_shard, cproj_shard = jnp.split(
        shared, [3 * half, 4 * half, 5 * half], axis=1
    )
    gather_self = gather(qkv_shard, proj_shard)
    gather_self.z_far()
    got_cols = lax.all_to_all(
        tie(packed, gather_self.mine), BOTH, split_axis=0, concat_axis=0, tiled=True
    )
    kv_shard = jnp.concatenate([tie(w_kv[0], gather_self.mine), w_kv[1]], axis=1)
    gather_one = gather(kv_shard, query_shard, cproj_shard)
    gather_one.z_far()
    frames_here = own_frames(tie(frames, gather_one.mine))
    gather_self.z_near(frames_here)
    gather_one.z_near(gather_self.two)
    gather_up = gather(tie(w_up, gather_one.two))
    gather_up.z_far()
    gather_self.landed(gather_up.mine)
    gather_self.across()
    got_cols = tie(got_cols, gather_self.first)
    ada_part = got_cols[:, :thin].reshape(width, ada_cols)
    digits = got_cols[:, thin, : 4 * ITEMS].astype(F32).reshape(n_dp, 2, 2, 2 * ITEMS)[:, 0]
    all_steps = (digits[:, 0] * 32.0 + digits[:, 1]).reshape(n_all * ITEMS)
    embedding = time_embed(all_steps, width)
    all_mods = jnp.dot(embedding, ada_part.astype(F32), precision=PRECISE)
    all_mods = all_mods.reshape(n_all, ITEMS, ada_cols)
    got_mods = lax.all_to_all(all_mods, BOTH, split_axis=0, concat_axis=0, tiled=True)
    ada_bias = got_cols[:, thin + 1, :bias_cols].reshape(9 * width).astype(F32)

    gather_one.landed(all_mods)
    gather_up.z_near(gather_one.first)
    gather_down = gather(tie(w_down, gather_up.two).T)
    gather_down.z_far()
    gather_self.corner(gather_up.two)
    gather_one.across(gather_self.second)
    item_mods = got_mods[:owners].transpose(1, 0, 2).reshape(ITEMS, 9 * width) + ada_bias

    text_rows = lax.dynamic_index_in_dim(text_states, core, 0, keepdims=False).reshape(ITEMS * TXT, width)
    residual = by_block(frames_here.astype(F32))
    grad_out = own_frames(tie(cotangent, all_mods))
    item_lengths, text_lengths = lax.optimization_barrier((item_lengths, text_lengths, all_mods))[:2]
    lengths = lax.dynamic_index_in_dim(item_lengths, core, 0, keepdims=False)[0]
    text_counts = lax.dynamic_index_in_dim(text_lengths, core, 0, keepdims=False)[0]

    item_count = jnp.sum((lengths > 0).astype(jnp.int32))
    nominal = SLAB // item_count
    slots = jnp.arange(ITEMS, dtype=jnp.int32)
    block_slot = (jnp.arange(BLOCKS, dtype=jnp.int32) * ROWS) // nominal
    block_hot = block_slot[:, None] == slots[None, :]
    position = jnp.arange(SLAB, dtype=jnp.int32)
    frame_slot = position // nominal
    own_length = jnp.sum(
        jnp.where(frame_slot[:, None] == slots[None, :], lengths[None, :], 0), axis=1
    )
    frame_live = position - frame_slot * nominal < own_length
    same = frame_slot[:, None] == frame_slot[None, :]
    self_bias = jnp.where(same & frame_live[None, :], 0.0, MASKED).astype(F32)
    self_bias_back = jnp.where(same & frame_live[:, None], 0.0, MASKED).astype(F32)
    text_live = jnp.arange(TXT, dtype=jnp.int32)[None, :] < text_counts[:, None]
    cross_bias = jnp.where(text_live, 0.0, MASKED).astype(F32)
    cross_bias_back = jnp.broadcast_to(cross_bias.reshape(ITEMS * TXT, 1), (ITEMS * TXT, ROWS))
    cross_bias = cross_bias[:, None, :]
    pairs = half // PAIR
    metas = [
        jnp.concatenate([block_slot, jnp.full((1,), pairs, jnp.int32) * side]).astype(jnp.int32)
        for side in (core, 1 - core)
    ]

    mods = jnp.sum(jnp.where(block_hot[:, :, None], item_mods[None], 0.0), axis=1)
    (
        shift_one,
        scale_one,
        gate_one,
        shift_two,
        scale_two,
        gate_two,
        shift_three,
        scale_three,
        gate_three,
    ) = [piece[:, None, :] for piece in jnp.split(mods, 9, axis=1)]

    def features_of(steps, side):
        column = lax.broadcasted_iota(jnp.int32, (1, thin + 1), 1)
        feature = (2 * dp + side) * thin + column
        return jnp.where(column < thin, time_features(steps, feature, width), 1.0)

    by_core = all_steps.reshape(n_dp, 2, ITEMS)
    slot_steps = pick((by_core[:, 0], by_core[:, 1])).reshape(n_dp * ITEMS)
    own_features, other_features = [features_of(slot_steps, side) for side in (core, 1 - core)]
    all_features = features_of(all_steps, core)

    norm_one, _ = normed(residual)
    hidden_one = flat(norm_one * (1.0 + scale_one) + shift_one).astype(BF16)
    w_qkvs, w_projs = gather_self.finish(hidden_one, gather_one.second)
    gather_one.corner(w_qkvs[0])
    gather_up.landed(gather_one.second)
    gather_up.across()
    projected = [mm(tie(hidden_one, gather_up.first), w_qkvs[0]).astype(BF16)]
    gather_down.z_near(projected[0])
    outs = [self_forward(tie(projected[0], gather_down.two), self_bias)]
    gather_down.landed(outs[0])
    projected.append(mm(tie(hidden_one, outs[0]), w_qkvs[1]).astype(BF16))
    outs.append(self_forward(projected[1], self_bias))
    w_kvs, w_queries, w_cprojs = gather_one.finish(outs[1])
    gather_up.corner(outs[1])
    gather_down.across(gather_up.second)
    attended = join(outs[0], tie(outs[1], w_kvs[0], gather_up.second), 1)
    proj_full = join(*w_projs, 1)
    branch_one = by_block(mm(attended, proj_full))
    after_one = residual + gate_one * branch_one
    norm_two, _ = normed(after_one)
    hidden_two = flat(norm_two * (1.0 + scale_two) + shift_two).astype(BF16)
    query_full, cproj_full = [join(*pair, 1) for pair in (w_queries, w_cprojs)]
    text_kv = mm(tie(text_rows, hidden_two), jnp.concatenate(w_kvs, axis=1)).astype(BF16)
    queries = mm(hidden_two, query_full).astype(BF16)
    crossed = cross_forward(metas[1], queries, text_kv, cross_bias)
    (w_ups,) = gather_up.finish(crossed)
    gather_down.corner(crossed)
    branch_two = by_block(mm(crossed, cproj_full))
    after_two = after_one + gate_two * branch_two
    norm_three, _ = normed(after_two)
    hidden_three = flat(norm_three * (1.0 + scale_three) + shift_three).astype(BF16)
    hidden_three = tie(hidden_three, gather_down.second)
    active, slopes = zip(*[gelu_parts(mm(hidden_three, weight)) for weight in w_ups])
    active, slopes = [[value.astype(BF16) for value in values] for values in (active, slopes)]
    (w_downs,) = gather_down.finish(active[0])
    branch_three = mm_tr(active[0], w_downs[0]) + mm_tr(active[1], w_downs[1])
    mods = mods[:, None, :]
    here = jnp.stack([core]).astype(jnp.int32)
    kept_out, sent_out, grad_down, sums_top = top_stage(here, grad_out, flat(after_two), branch_three, mods)
    got_out = swap_core(sent_out)

    def columns(values):
        return [part(values, half, core, 1), part(values, half, 1 - core, 1)]

    def by_item(*grads):
        grads = jnp.concatenate(grads, axis=1).reshape(BLOCKS, -1)
        return jnp.sum(jnp.where(block_hot[:, :, None], grads[:, None, :], 0.0), axis=0).astype(BF16)

    def to_all(items, axes, count):
        copies = jnp.broadcast_to(items[None], (count,) + items.shape)
        return copies, lax.all_to_all(copies, axes, split_axis=0, concat_axis=0, tiled=True)

    def ada_rows(features, items):
        items = items.reshape(features.shape[0], -1).astype(F32)
        return lax.dot_general(
            features, items, (((0,), (0,)), ((), ())), precision=PRECISE, preferred_element_type=F32
        )

    sum_ff, sum_cross, sum_self = [Scatter(dp, core, n_dp) for _ in range(3)]

    sent = sum_ff.add(grad_down, active[0], active[1])
    grad_ups = [
        (mm(tie(grad_down, sent), weight) * slope.astype(F32)).astype(BF16)
        for weight, slope in zip(w_downs, slopes)
    ]
    sent = sum_ff.add(hidden_three, grad_ups[0], grad_ups[1])
    grad_ups = [tie(grad, sent) for grad in grad_ups]
    grad_hidden = mm_tr(grad_ups[0], w_ups[0]) + mm_tr(grad_ups[1], w_ups[1])

    grad_two, grad_cproj, sums_three = middle_stage(
        here, grad_hidden, flat(after_two), grad_out, flat(branch_two), mods, 2
    )
    sums = sum_ff.chip(grad_cproj)
    grad_crossed = mm_tr(tie(grad_cproj, *sums), cproj_full).astype(BF16)
    block_out = both(kept_out, got_out)
    sent = sum_ff.across(grad_crossed, block_out)
    grad_crossed = tie(grad_crossed, sent)
    grad_query, grad_kvs = cross_backward(metas[1], queries, text_kv, grad_crossed, cross_bias_back)
    sum_cross.add(crossed, *columns(grad_cproj))
    sum_cross.add(hidden_two, *columns(grad_query))
    sent = sum_cross.add(text_rows, grad_kvs[0], grad_kvs[1])
    grad_hidden = mm_tr(tie(grad_query, sent), query_full)

    grad_one, grad_proj, sums_two = middle_stage(
        here, grad_hidden, flat(after_one), grad_two, flat(branch_one), mods, 1
    )
    sums = sum_cross.chip(grad_proj)
    sent = sum_ff.corner(*sums)
    grad_proj = tie(grad_proj, sent)
    sent = sum_cross.add(attended, *columns(grad_proj))
    grad_attended = mm_tr(tie(grad_proj, sent), proj_full).astype(BF16)
    grad_kvs = tie(grad_kvs, grad_attended)
    grad_text = (mm_tr(grad_kvs[0], w_kvs[0]) + mm_tr(grad_kvs[1], w_kvs[1])).astype(BF16)
    text_halves = halves(grad_text.reshape(ITEMS, TXT, width), 1)
    early_items = by_item(
        sums_two[:, 2:], sums_two[:, :2], sums_three[:, 2:], sums_three[:, :2], sums_top
    )
    early_copies, early_items = to_all(early_items, "dp", n_dp)
    sum_cross.chip(text_halves[0])
    sent = sum_cross.across(grad_attended, early_copies)
    sent = sum_ff.z_near(sent)
    other = self_backward(metas[1], projected[1], tie(grad_attended, sent), self_bias_back)
    sent = sum_cross.corner(other)
    other = tie(other, sent)
    crossing = mm_tl(hidden_one, other).astype(BF16)
    sent = sum_ff.z_far(crossing)
    own = self_backward(metas[0], projected[0], tie(grad_attended, sent), self_bias_back)
    sum_self.totals.append([mm_tl(hidden_one, own).astype(BF16), swap_core(crossing)])
    sent = sum_self.across()
    own, other = lax.optimization_barrier((own, other, sent))[:2]
    grad_hidden = mm_tr(own, w_qkvs[0]) + mm_tr(other, w_qkvs[1])
    sent = sum_cross.z_near(grad_hidden)
    text_grad = both(tie(text_halves[0], grad_hidden), text_halves[1]).astype(F32)
    sent = sum_self.corner(grad_hidden, sent, text_grad)
    grad_hidden = tie(grad_hidden, sent)
    kept_in, sent_in, sums_one = bottom_stage(here, grad_hidden, frames_here, grad_one, mods)
    got_in = swap_core(sent_in)

    late_copies, late_items = to_all(by_item(sums_one), BOTH, n_all)
    sent = sum_self.z_near(late_copies)
    sent = sum_cross.z_far(sent)
    early_items = tie(early_items, sent)
    early_rows = ada_rows(own_features, early_items)
    early_sent = ada_rows(other_features, early_items)
    sent = sum_self.z_far(early_sent)
    frames_grad = both(tie(kept_in, sent), got_in)
    late_rows = ada_rows(all_features, tie(late_items, sent))
    ada_sum = jnp.concatenate([late_rows, early_rows + swap_core(early_sent)], axis=1)
    bias_sum = lax.dynamic_slice_in_dim(ada_sum[thin], (2 * dp + core) * bias_cols, bias_cols, 0)
    ada_sum = ada_sum[:thin]

    def own_rows(values):
        kept = part(values, thin, core, 0)
        got = swap_core(part(values, thin, 1 - core, 0))
        return join(kept, got, 1)

    ff_sum = sum_ff.finish(own)
    down_sum, up_sum = jnp.split(ff_sum, [2 * width], axis=1)
    cross_sum = sum_cross.finish(sent)
    cproj_part, query_part, kv_part, proj_part = jnp.split(
        cross_sum, [half, 2 * half, 4 * half], axis=1
    )
    kv_grad = jnp.stack(jnp.split(kv_part, 2, axis=1))
    qkv_grad = own_rows(sum_self.finish(frames_grad, ada_sum, bias_sum))
    qkv_grad = qkv_grad.reshape(thin, 2, 3, half).transpose(0, 2, 1, 3).reshape(thin, 3 * width)
    return (
        block_out,
        frames_grad,
        text_grad[:, None],
        qkv_grad,
        own_rows(proj_part),
        own_rows(query_part),
        own_rows(cproj_part),
        ada_sum,
        bias_sum,
        kv_grad,
        up_sum,
        down_sum.T,
    )


def solution(mesh):
    return jax.shard_map(
        per_device,
        mesh=mesh,
        in_specs=(
            P(None, ("dp", "head"), None),
            P(None, "dp", None, None, None),
            P(None, ("dp", "head"), None),
            P(None, "dp", None),
            P(None, "dp", None),
            P(None, "dp", None),
            P(("dp", "head"), None),
            P(("dp", "head"), None),
            P(("dp", "head"), None),
            P(("dp", "head"), None),
            P(("dp", "head"), None),
            P(("dp", "head")),
            P(None, "dp", "head"),
            P("dp", "head"),
            P("head", "dp"),
        ),
        out_specs=(
            P(None, ("dp", "head"), None),
            P(None, ("dp", "head"), None),
            P(None, "dp", None, "head", None),
            P(("dp", "head"), None),
            P(("dp", "head"), None),
            P(("dp", "head"), None),
            P(("dp", "head"), None),
            P(("dp", "head"), None),
            P(("dp", "head")),
            P(None, "dp", "head"),
            P("dp", "head"),
            P("head", "dp"),
        ),
        check_vma=False,
    )
```
